32 devices in a mesh: grp: 2 (over y), row: 4 (over x, core), col: 4 (over z).
Axes of the slice: x: 2, y: 2, z: 4, core: 2. Of those that a mesh axis runs over, the one named last changes fastest.
Arguments:
- values: bfloat16 [8, 4, 2, 27, 128, 128], P(('grp', 'row'), 'col'), parts along dimension 0, may hold values from -0.59765625 to 0.59765625
- pattern: int32 [8, 4, 2, 27], P(('grp', 'row'), 'col'), parts along dimension 0, may hold values from 0 to 1, as said below
Outputs:
- purified: bfloat16 [8, 4, 2, 27, 128, 128], P(('grp', 'row'), 'col'), parts along dimension 0
The draws below stay inside these ranges and needn't reach their ends.
There are 2 independent parts, one for each index of `grp`. The reference program is written for one: setup_inputs(seed, part) draws one part's arguments, and reference() takes and returns one part's arrays. A program takes and returns all parts, laid end to end along the dimension named above; each array names one. Nothing has to cross between parts.
Inputs may be any that keep to these rules, and one draw needn't show every extreme that they name: pattern[x, y, z, 13] = 1 (the cell's own block) everywhere; pattern[x, y, z, k] = 0 wherever z plus the z offset of slot k leaves 0 to 1; every other entry is 0 or 1.
All inputs are finite; a program needn't handle non-finite values.
Results may differ from the reference program's by a relative error of at most 0.005.
Values may be sent and summed in bfloat16 or wider, within the bound.
No kernel may reach another device: no remote copies, remote signals or barrier semaphores. Data moves between devices by JAX's collectives and lax.ppermute only.
A program may use at most 64 MiB of HBM per device.

```python
import jax
import jax.numpy as jnp
import numpy as np
from jax import lax

B = 128
K = 27
LZ = 2
LX = 4
LY = 4


def depth_offsets():
    offset_list = []
    for along_x in (-1, 0, 1):
        for along_y in (-1, 0, 1):
            for along_z in (-1, 0, 1):
                offset_list.append(along_z)
    return np.array(offset_list, np.int32)


def draw_pattern(key, part):
    key = jax.random.fold_in(key, 5)
    levels = jax.random.randint(key, (LX, LY, LZ, K), 0, 20)
    present = (levels < 17).astype(jnp.int32)
    slot_ids = jnp.arange(K, dtype=jnp.int32)
    present = jnp.where(slot_ids == 13, 1, present)
    reached = jnp.arange(LZ, dtype=jnp.int32)[:, None] + jnp.asarray(depth_offsets())[None, :]
    inside = (reached >= 0) & (reached < LZ)
    return jnp.where(inside[None, None], present, 0).astype(jnp.int32)


def shard_levels(key, dims, shards, smallest, high):
    def one(dim, blocks):
        draws = jax.random.uniform(jax.random.fold_in(jax.random.fold_in(key, 6), dim), (blocks,), jnp.float32, smallest / len(shards), high / len(shards))
        return jnp.repeat(jnp.exp(draws), dims[dim] // blocks).reshape((-1,) + (1,) * (len(dims) - dim - 1))

    factor_of = one(*shards[0])
    for cut in shards[1:]:
        factor_of = factor_of * one(*cut)
    return factor_of


def normal_values(own_key, dims, scale, limit, pieces=(), kind=jnp.bfloat16):
    entries = scale * jax.random.normal(own_key, dims, jnp.float32)
    if pieces:
        entries = entries * shard_levels(own_key, dims, pieces, -0.22, 0.18)
    return jnp.clip(entries, -limit, limit).astype(kind)


def setup_inputs(seed: int = 0, part: int = 0) -> dict:
    streams_of = jax.random.split(jax.random.key(seed), 3)
    part_keys = jax.random.split(jax.random.fold_in(streams_of[2], part), 3)
    values = normal_values(part_keys[0], (LX, LY, LZ, K, B, B), 0.1, 0.59765625, ((0, 4), (1, 4)))
    pattern = draw_pattern(jax.random.fold_in(jax.random.fold_in(streams_of[2], part), 71), part)
    return {"values": values, "pattern": pattern}


def slot_offsets():
    offset_list = []
    for along_x in (-1, 0, 1):
        for along_y in (-1, 0, 1):
            for along_z in (-1, 0, 1):
                offset_list.append((along_x, along_y, along_z))
    return offset_list


def pair_groups():
    offset_list = slot_offsets()
    position = {}
    for slot_id, offset in enumerate(offset_list):
        position[offset] = slot_id
    groups = []
    for wanted in offset_list:
        members = []
        for left_slot, shift_vector in enumerate(offset_list):
            remainder = tuple(wanted[axis_id] - shift_vector[axis_id] for axis_id in range(3))
            if remainder in position:
                members.append((left_slot, position[remainder]))
        groups.append(members)
    return groups


def shifted(right_side, along_x, along_y, along_z, right_slot):
    column_block = right_side[:, :, :, right_slot]
    column_block = jnp.roll(column_block, (-along_x, -along_y), axis=(0, 1))
    thickness = column_block.shape[2]
    padded = jnp.pad(column_block, ((0, 0), (0, 0), (1, 1), (0, 0), (0, 0)))
    return lax.slice_in_dim(padded, 1 + along_z, 1 + along_z + thickness, axis=2)


def restricted(left_side, right_side, pattern):
    offset_list = slot_offsets()
    columns = []
    for members in pair_groups():
        totals = jnp.zeros(left_side.shape[:3] + left_side.shape[4:], jnp.float32)
        for left_slot, right_slot in members:
            along_x, along_y, along_z = offset_list[left_slot]
            factor = shifted(right_side, along_x, along_y, along_z, right_slot)
            totals = totals + jnp.einsum("xyzpq,xyzqr->xyzpr", left_side[:, :, :, left_slot].astype(jnp.float32), factor.astype(jnp.float32))
        columns.append(totals)
    stacked = jnp.stack(columns, axis=3)
    return stacked * pattern[..., None, None].astype(jnp.float32)


def reference(values, pattern):
    matrix = values * pattern[..., None, None].astype(jnp.bfloat16)
    square = restricted(matrix, matrix, pattern).astype(jnp.bfloat16)
    square = lax.optimization_barrier(square)
    cubic = restricted(square, matrix, pattern)
    combined = (3.0 * square.astype(jnp.float32) - 2.0 * cubic) * pattern[..., None, None].astype(jnp.float32)
    return combined.astype(jnp.bfloat16)
```

```python
import functools

import jax
import jax.numpy as jnp
from jax import lax
from jax.experimental import pallas as pl
from jax.experimental.pallas import tpu as pltpu
from jax.sharding import PartitionSpec as P

STEPS = (-1, 0, 1)


def tile_index(along_u, along_y):
    return (along_u + 1) * 3 + along_y + 1


def pack_kernel(flip, keep, values, mat, x_out, n_out, *z_out):
    width = values.shape[-1]
    sign = flip[0]
    z_up = dict(zip((0, 1, -1), z_out[:3]))
    z_down = dict(zip((0, 1, -1), z_out[3:]))
    for along_u in (0, 1, -1):
        for along_y in STEPS:
            base = 3 * ((sign * along_u + 1) * 3 + along_y + 1) + 1
            targets = [mat.at[tile_index(along_u, along_y)]]
            if along_u >= 0:
                targets.append(x_out.at[along_u * 3 + along_y + 1])
            if along_u <= 0:
                targets.append(n_out.at[-along_u * 3 + along_y + 1])
            if along_y >= 0:
                targets.append(z_up[along_u].at[along_y])
            if along_y <= 0:
                targets.append(z_down[along_u].at[along_y + 1])
            for low in range(2):
                for high in range(2):
                    slot = base + high - low
                    block = values[low, slot] * keep[low, slot].astype(jnp.float32).astype(values.dtype)
                    for target in targets:
                        target[pl.ds(low * width, width), pl.ds(high * width, width)] = block


def product_kernel(flip, keep, mat, x_in, n_in, *rest):
    zu = dict(zip((0, 1, -1), rest[0:3]))
    zd = dict(zip((0, 1, -1), rest[3:6]))
    xu = dict(zip((0, 1), rest[6:8]))
    xd = dict(zip((0, 1), rest[8:10]))
    nu = dict(zip((0, -1), rest[10:12]))
    nd = dict(zip((0, -1), rest[12:14]))
    out, square = rest[14:]
    width = out.shape[-1]
    sign = flip[0]

    def factor(a, c):
        (au, ay), (cu, cy) = a, c
        if au == 0 and ay == 0:
            return mat[tile_index(cu, cy)]
        if ay == 0:
            return (x_in if au > 0 else n_in)[abs(cu) * 3 + cy + 1]
        if au == 0:
            return (zu if ay < 0 else zd)[cu][cy if ay < 0 else cy + 1]
        if au > 0:
            return (xu if ay < 0 else xd)[-cu][cy if ay < 0 else cy + 1]
        return (nu if ay < 0 else nd)[-cu][cy if ay < 0 else cy + 1]

    def total(left, b):
        lefts, rights = [], []
        for au in STEPS:
            for ay in STEPS:
                c = (b[0] - au, b[1] - ay)
                if abs(c[0]) <= 1 and abs(c[1]) <= 1:
                    lefts.append(left[tile_index(au, ay)])
                    rights.append(factor((au, ay), c))
        return jnp.dot(
            jnp.concatenate(lefts, axis=1), jnp.concatenate(rights, axis=0), preferred_element_type=jnp.float32
        )

    def slots(b):
        base = 3 * ((sign * b[0] + 1) * 3 + b[1] + 1) + 1
        for low in range(2):
            for high in range(2):
                slot = base + high - low
                yield low, high, slot, keep[low, slot].astype(jnp.float32)

    cells = [(bu, by) for bu in STEPS for by in STEPS]
    for b in cells:
        summed = total(mat, b)
        for low, high, slot, kept in slots(b):
            quarter = summed[low * width : (low + 1) * width, high * width : (high + 1) * width] * kept
            square[tile_index(*b), pl.ds(low * width, width), pl.ds(high * width, width)] = quarter.astype(jnp.bfloat16)
    for b in cells:
        summed = total(square, b)
        own = square[tile_index(*b)].astype(jnp.float32)
        for low, high, slot, kept in slots(b):
            rows, columns = slice(low * width, (low + 1) * width), slice(high * width, (high + 1) * width)
            mixed = (3.0 * own[rows, columns] - 2.0 * summed[rows, columns]) * kept
            out[low, slot] = mixed.astype(out.dtype)
    empty = jnp.zeros((width, width), out.dtype)
    for m in range(9):
        out[0, 3 * m] = empty
        out[1, 3 * m + 2] = empty


def local(values, pattern):
    blocks, keep = values[0, 0], pattern[0, 0]
    dtype, width = blocks.dtype, blocks.shape[-1]
    side = 2 * width
    rows, cols = lax.axis_size("row"), lax.axis_size("col")
    flip = (2 * lax.rem(lax.axis_index("row"), 2) - 1).reshape(1)

    near, far = [], []
    for i in range(0, rows, 2):
        near += [(i, i + 1), (i + 1, i)]
        far += [(i + 1, (i + 2) % rows), ((i + 2) % rows, i + 1)]
    up = [(i, (i + 1) % cols) for i in range(cols)]
    down = [(i, (i - 1) % cols) for i in range(cols)]

    def tiles(count):
        return jax.ShapeDtypeStruct((count, side, side), dtype)

    smem = pl.BlockSpec(memory_space=pltpu.SMEM)
    vmem = pl.BlockSpec(memory_space=pltpu.VMEM)
    mat, x_out, n_out, *z_out = pl.pallas_call(
        pack_kernel,
        out_shape=[tiles(9), tiles(6), tiles(6)] + [tiles(2)] * 6,
        in_specs=[smem, smem, vmem],
        out_specs=[vmem] * 9,
        compiler_params=pltpu.CompilerParams(vmem_limit_bytes=16 << 20),
        name="pack",
    )(flip, keep, blocks)

    x_in = lax.ppermute(x_out, "row", far)
    zu0 = lax.ppermute(z_out[0], "col", up)
    zd0 = lax.ppermute(z_out[3], "col", down)
    zu1 = lax.ppermute(z_out[1], "col", up)
    zd1 = lax.ppermute(z_out[4], "col", down)
    xu0 = lax.ppermute(zu0, "row", far)
    xd0 = lax.ppermute(zd0, "row", far)
    zu2 = lax.ppermute(z_out[2], "col", up)
    zd2 = lax.ppermute(z_out[5], "col", down)
    xu1 = lax.ppermute(zu1, "row", far)
    xd1 = lax.ppermute(zd1, "row", far)
    n_in = lax.ppermute(n_out, "row", near)
    nu0 = lax.ppermute(zu0, "row", near)
    nd0 = lax.ppermute(zd0, "row", near)
    nu2 = lax.ppermute(zu2, "row", near)
    nd2 = lax.ppermute(zd2, "row", near)

    purified = pl.pallas_call(
        product_kernel,
        out_shape=jax.ShapeDtypeStruct(blocks.shape, dtype),
        in_specs=[smem, smem] + [vmem] * 17,
        out_specs=vmem,
        scratch_shapes=[pltpu.VMEM((9, side, side), dtype)],
        compiler_params=pltpu.CompilerParams(vmem_limit_bytes=24 << 20),
        name="product",
    )(flip, keep, mat, x_in, n_in, zu0, zu1, zu2, zd0, zd1, zd2, xu0, xu1, xd0, xd1, nu0, nu2, nd0, nd2)
    return purified[None, None]


def solution(mesh):
    return jax.shard_map(
        local,
        mesh=mesh,
        in_specs=(
            P(("grp", "row"), "col", None, None, None, None),
            P(("grp", "row"), "col", None, None),
        ),
        out_specs=P(("grp", "row"), "col", None, None, None, None),
        check_vma=False,
    )
```

```python
import functools

import jax
import jax.numpy as jnp
from jax import lax
from jax.experimental import pallas as pl
from jax.experimental.pallas import tpu as pltpu
from jax.sharding import PartitionSpec as P

STEPS = (-1, 0, 1)


def tile_index(along_u, along_y):
    return (along_u + 1) * 3 + along_y + 1


def pack_kernel(flip, keep, values, mat, x_out, n_out, up_out, up_last, *down_out):
    width = values.shape[-1]
    sign = flip[0]
    for along_u in (0, 1, -1):
        for along_y in STEPS:
            base = 3 * ((sign * along_u + 1) * 3 + along_y + 1) + 1
            targets = [mat.at[tile_index(along_u, along_y)]]
            if along_u >= 0:
                targets.append(x_out.at[along_u * 3 + along_y + 1])
            if along_u <= 0:
                targets.append(n_out.at[-along_u * 3 + along_y + 1])
            if along_y >= 0:
                targets.append(up_last.at[along_y] if along_u < 0 else up_out.at[along_u * 2 + along_y])
            if along_y <= 0:
                targets.append(down_out[along_u % 3].at[along_y + 1])
            for low in range(2):
                for high in range(2):
                    slot = base + high - low
                    block = values[low, slot] * keep[low, slot].astype(jnp.float32).astype(values.dtype)
                    for target in targets:
                        target[pl.ds(low * width, width), pl.ds(high * width, width)] = block


def product_kernel(flip, keep, mat, x_in, n_in, up_in, up_rest, x_up, n_up, n_up_rest, *rest):
    down_in, x_down, n_down = rest[0:3], rest[3:5], rest[5:7]
    out, square = rest[7:]
    width = out.shape[-1]
    sign = flip[0]

    def factor(a, c):
        (au, ay), (cu, cy) = a, c
        if au == 0 and ay == 0:
            return mat[tile_index(cu, cy)]
        if ay == 0:
            return (x_in if au > 0 else n_in)[abs(cu) * 3 + cy + 1]
        if ay > 0:
            source = down_in[cu % 3] if au == 0 else x_down[-cu] if au > 0 else n_down[cu]
            return source[cy + 1]
        if au > 0:
            return x_up[-cu * 2 + cy]
        if cu * (1 + au) < 0 or cu > 0 > au:
            return (up_rest if au == 0 else n_up_rest)[cy]
        return (up_in if au == 0 else n_up)[cu * (1 + au) * 2 + cy]

    def total(left, b):
        lefts, rights = [], []
        for au in STEPS:
            for ay in STEPS:
                c = (b[0] - au, b[1] - ay)
                if abs(c[0]) <= 1 and abs(c[1]) <= 1:
                    lefts.append(left[tile_index(au, ay)])
                    rights.append(factor((au, ay), c))
        return jnp.dot(
            jnp.concatenate(lefts, axis=1), jnp.concatenate(rights, axis=0), preferred_element_type=jnp.float32
        )

    def slots(b):
        base = 3 * ((sign * b[0] + 1) * 3 + b[1] + 1) + 1
        for low in range(2):
            for high in range(2):
                slot = base + high - low
                yield low, high, slot, keep[low, slot].astype(jnp.float32)

    cells = [(bu, by) for bu in STEPS for by in STEPS]
    for b in cells:
        summed = total(mat, b)
        for low, high, slot, kept in slots(b):
            quarter = summed[low * width : (low + 1) * width, high * width : (high + 1) * width] * kept
            square[tile_index(*b), pl.ds(low * width, width), pl.ds(high * width, width)] = quarter.astype(jnp.bfloat16)
    for b in cells:
        summed = total(square, b)
        own = square[tile_index(*b)].astype(jnp.float32)
        for low, high, slot, kept in slots(b):
            rows, columns = slice(low * width, (low + 1) * width), slice(high * width, (high + 1) * width)
            mixed = (3.0 * own[rows, columns] - 2.0 * summed[rows, columns]) * kept
            out[low, slot] = mixed.astype(out.dtype)
    empty = jnp.zeros((width, width), out.dtype)
    for m in range(9):
        out[0, 3 * m] = empty
        out[1, 3 * m + 2] = empty


def local(values, pattern):
    blocks, keep = values[0, 0], pattern[0, 0]
    dtype, width = blocks.dtype, blocks.shape[-1]
    side = 2 * width
    rows, cols = lax.axis_size("row"), lax.axis_size("col")
    flip = (2 * lax.rem(lax.axis_index("row"), 2) - 1).reshape(1)

    near, far = [], []
    for i in range(0, rows, 2):
        near += [(i, i + 1), (i + 1, i)]
        far += [(i + 1, (i + 2) % rows), ((i + 2) % rows, i + 1)]
    up = [(i, (i + 1) % cols) for i in range(cols)]
    down = [(i, (i - 1) % cols) for i in range(cols)]

    def tiles(count):
        return jax.ShapeDtypeStruct((count, side, side), dtype)

    smem = pl.BlockSpec(memory_space=pltpu.SMEM)
    vmem = pl.BlockSpec(memory_space=pltpu.VMEM)
    mat, x_out, n_out, up_out, up_last, down0, down1, down2 = pl.pallas_call(
        pack_kernel,
        out_shape=[tiles(9), tiles(6), tiles(6), tiles(4)] + [tiles(2)] * 4,
        in_specs=[smem, smem, vmem],
        out_specs=[vmem] * 8,
        compiler_params=pltpu.CompilerParams(vmem_limit_bytes=16 << 20),
        name="pack",
    )(flip, keep, blocks)

    def along_col(tile, towards):
        return lax.ppermute(tile, "col", towards)

    def along_row(tile, towards):
        return lax.ppermute(tile, "row", towards)

    after = lax.optimization_barrier
    x_in = along_row(x_out, far)
    up_in, up_rest = along_col(up_out, up), along_col(up_last, up)
    up_in, down0, down1 = after((up_in, down0, down1))
    x_up = along_row(up_in, far)
    down0, down1 = along_col(down0, down), along_col(down1, down)
    x_in, down2 = after((x_in, down2))
    down2 = along_col(down2, down)
    x_down0 = along_row(down0, far)
    x_up, down1 = after((x_up, down1))
    x_down1 = along_row(down1, far)
    down0, n_out, up_in = after((down0, n_out, up_in))
    n_in, n_up = along_row(n_out, near), along_row(up_in, near)
    down1, down0 = after((down1, down0))
    n_down0 = along_row(down0, near)
    x_down0, down2, up_rest = after((x_down0, down2, up_rest))
    n_down2, n_up_rest = along_row(down2, near), along_row(up_rest, near)

    purified = pl.pallas_call(
        product_kernel,
        out_shape=jax.ShapeDtypeStruct(blocks.shape, dtype),
        in_specs=[smem, smem] + [vmem] * 15,
        out_specs=vmem,
        scratch_shapes=[pltpu.VMEM((9, side, side), dtype)],
        compiler_params=pltpu.CompilerParams(vmem_limit_bytes=24 << 20),
        name="product",
    )(
        flip, keep, mat, x_in, n_in, up_in, up_rest, x_up, n_up, n_up_rest,
        down0, down1, down2, x_down0, x_down1, n_down0, n_down2,
    )
    return purified[None, None]


def solution(mesh):
    return jax.shard_map(
        local,
        mesh=mesh,
        in_specs=(
            P(("grp", "row"), "col", None, None, None, None),
            P(("grp", "row"), "col", None, None),
        ),
        out_specs=P(("grp", "row"), "col", None, None, None, None),
        check_vma=False,
    )
```

```python
import jax
import jax.numpy as jnp
from jax import lax
from jax.experimental import pallas as pl
from jax.experimental.pallas import tpu as pltpu
from jax.sharding import PartitionSpec as P

STEPS = (-1, 0, 1)
CELLS = [(along_u, along_y) for along_u in STEPS for along_y in STEPS]
EDGES = {
    1: {"in": [(u, y) for u in (0, 1) for y in STEPS]},
    -1: {"in": [(u, y) for u in (0, -1) for y in STEPS]},
}
PIECES = {
    1: {"up": [(0, 0), (0, 1), (1, 0), (1, 1)], "up_rest": [(-1, 0), (-1, 1)]},
    -1: {"down0": [(0, -1), (0, 0)], "down1": [(1, -1), (1, 0)], "down2": [(-1, -1), (-1, 0)]},
}
STAGES = [['mat', 'x_in', 'up', 'x_up', 'down1'],
 ['up_rest', 'down2', 'x_down0', 'x_down1', 'n_in', 'n_up', 'n_down0', 'n_down2', 'n_up_rest', 'down0']]
SCHEDULE = [('x_in', []), ('up', []), ('x_up', []), ('down0', ['up']), ('down1', ['up']), (0, []), ('up_rest', ['x_in']),
 ('down2', ['x_in']), ('x_down0', []), ('x_down1', ['x_up']), ('n_in', ['down0']), ('n_up', ['down0']),
 ('n_down0', ['sum_0']), ('n_down2', ['sum_0']), ('n_up_rest', ['down1', 'n_up', 'sum_0', 'x_down0']),
 (1, [])]
FLOPS = [1, 1]


def holder(a, c):
    (au, ay), (cu, cy) = a, c
    if au == 0 and ay == 0:
        return "mat", CELLS.index(c)
    prefix = {0: "", 1: "x_", -1: "n_"}[au]
    wanted = (cu if au == 0 else -cu, cy)
    for name, tiles in (EDGES[au] if ay == 0 else PIECES[-ay]).items():
        if wanted in tiles:
            return prefix + name, tiles.index(wanted)


def pairs(b):
    for a in CELLS:
        c = (b[0] - a[0], b[1] - a[1])
        if abs(c[0]) <= 1 and abs(c[1]) <= 1:
            yield a, holder(a, c)


def stage_plan():
    stage_of = {name: k for k, names in enumerate(STAGES) for name in names}
    whole = {b: max(stage_of[name] for _, (name, _) in pairs(b)) for b in CELLS}
    plan = []
    for k in range(len(STAGES)):
        squares = {b: [p for p in pairs(b) if stage_of[p[1][0]] == k] for b in CELLS}
        cubics = {b: [p for p in pairs(b) if max(stage_of[p[1][0]], whole[p[0]]) == k] for b in CELLS}
        plan.append(
            (
                {b: chosen for b, chosen in squares.items() if chosen},
                [b for b in CELLS if whole[b] == k],
                {b: chosen for b, chosen in cubics.items() if chosen},
            )
        )
    return plan


def total(lefts, rights, base):
    summed = jnp.dot(
        jnp.concatenate(lefts, axis=1), jnp.concatenate(rights, axis=0), preferred_element_type=jnp.float32
    )
    return summed if base is None else base + summed


def first_slot(b, sign):
    return 3 * ((sign * b[0] + 1) * 3 + b[1] + 1)


def quarters(b, sign, keep, width):
    for low in range(2):
        for high in range(2):
            rows, columns = slice(low * width, (low + 1) * width), slice(high * width, (high + 1) * width)
            yield low, high, rows, columns, keep[low, first_slot(b, sign) + 1 + high - low].astype(jnp.float32)


def pack_kernel(layout, flip, keep, values, *outs):
    width = values.shape[-1]
    sign = flip[0]
    for b in CELLS:
        targets = [out.at[tiles.index(b)] for out, tiles in zip(outs, layout) if b in tiles]
        for low, high, rows, columns, kept in quarters(b, sign, keep, width):
            block = values[low, first_slot(b, sign) + 1 + high - low] * kept.astype(values.dtype)
            for target in targets:
                target[rows, columns] = block


def product_kernel(work, names, found, made, flip, keep, *refs):
    squares, finished, cubics, final = work
    inputs, refs = dict(zip(names, refs)), refs[len(names) :]
    outputs = dict(zip(made["arrays"], refs))
    sign = flip[0]

    def put(kind, b, value):
        name, place = made[kind, b]
        outputs[name][place] = value.astype(outputs[name].dtype)

    def get(kind, b):
        name, place = made[kind, b] if kind == "square" and ("square", b) in made else found[kind, b]
        return (outputs if name in outputs else inputs)[name][place]

    for b in CELLS:
        if b in squares or b in finished:
            base = get("sum", b) if ("sum", b) in found else None
            chosen = squares.get(b, [])
            value = base
            if chosen:
                lefts = [inputs["mat"][CELLS.index(a)] for a, _ in chosen]
                value = total(lefts, [inputs[name][place] for _, (name, place) in chosen], base)
            if b not in finished:
                put("sum", b, value)
                continue
            name, place = made["square", b]
            width = value.shape[-1] // 2
            for _, _, rows, columns, kept in quarters(b, sign, keep, width):
                outputs[name][place, rows, columns] = (value[rows, columns] * kept).astype(outputs[name].dtype)
    if final:
        out, stage, copied = refs[len(outputs) :]
        width = out.shape[-1]
        empty = jnp.zeros((width, width), out.dtype)
        copies = []
    for b in CELLS:
        chosen = cubics.get(b, [])
        if not chosen and not final:
            continue
        value = get("cubic", b) if ("cubic", b) in found else None
        if chosen:
            lefts = [get("square", a) for a, _ in chosen]
            value = total(lefts, [inputs[name][place] for _, (name, place) in chosen], value)
        if not final:
            put("cubic", b, value)
            continue
        own = get("square", b).astype(jnp.float32)
        cell = CELLS.index(b)
        for low, high, rows, columns, kept in quarters(b, sign, keep, width):
            mixed = (3.0 * own[rows, columns] - 2.0 * value[rows, columns]) * kept
            stage[cell, low, 1 + high - low] = mixed.astype(out.dtype)
        for low in range(2):
            stage[cell, low, 2 * low] = empty
            copies.append(
                pltpu.make_async_copy(
                    stage.at[cell, low], out.at[low, pl.ds(first_slot(b, sign), 3)], copied.at[cell, low]
                )
            )
            copies[-1].start()
    if final:
        for copy in copies:
            copy.wait()


def local(values, pattern):
    blocks, keep = values[0, 0], pattern[0, 0]
    dtype, width = blocks.dtype, blocks.shape[-1]
    side = 2 * width
    rows, cols = lax.axis_size("row"), lax.axis_size("col")
    flip = (2 * lax.rem(lax.axis_index("row"), 2) - 1).reshape(1)

    near, far = [], []
    for i in range(0, rows, 2):
        near += [(i, i + 1), (i + 1, i)]
        far += [(i + 1, (i + 2) % rows), ((i + 2) % rows, i + 1)]
    up = [(i, (i + 1) % cols) for i in range(cols)]
    down = [(i, (i - 1) % cols) for i in range(cols)]

    def tiles(count, kind=dtype):
        return jax.ShapeDtypeStruct((count, side, side), kind)

    smem = pl.BlockSpec(memory_space=pltpu.SMEM)
    vmem = pl.BlockSpec(memory_space=pltpu.VMEM)
    hbm = pl.BlockSpec(memory_space=pltpu.HBM)

    sent = {name: (held, "col", up) for name, held in PIECES[1].items()}
    sent |= {name: (held, "col", down) for name, held in PIECES[-1].items()}
    sent |= {"x_" + name: (held, "row", far) for name, held in EDGES[1].items()}
    sent |= {"n_" + name: (held, "row", near) for name, held in EDGES[-1].items()}
    layout = [CELLS] + [held for held, _, _ in sent.values()]
    packed = pl.pallas_call(
        lambda *refs: pack_kernel(layout, *refs),
        out_shape=[tiles(len(held)) for held in layout],
        in_specs=[smem, smem, vmem],
        out_specs=[vmem] * len(layout),
        compiler_params=pltpu.CompilerParams(vmem_limit_bytes=16 << 20),
        name="pack",
    )(flip, keep, blocks)
    ready = dict(zip(sent, packed[1:]))
    arrays = {"mat": packed[0]}
    plan, found = stage_plan(), {}

    def move(name, gates):
        if name in sent:
            operand, (_, axis, towards) = ready[name], sent[name]
        else:
            operand, axis, towards = arrays[name[2:]], "row", far if name[0] == "x" else near
        gates = [gate for gate in gates if name in sent or gate != name[2:]]
        if gates:
            operand, *held = lax.optimization_barrier((operand, *(arrays[gate] for gate in gates)))
            arrays.update(zip(gates, held))
            if name not in sent:
                arrays[name[2:]] = operand
        arrays[name] = lax.ppermute(operand, axis, towards)

    def multiply(k):
        squares, finished, cubics = plan[k]
        final = k == len(plan) - 1
        names = {"mat"} | {name for chosen in (*squares.values(), *cubics.values()) for _, (name, _) in chosen}
        used = [("sum", b) for b in CELLS if b in squares or b in finished]
        used += [("square", a) for chosen in cubics.values() for a, _ in chosen]
        used += [("square", b) for b in CELLS if final] + [("cubic", b) for b in CELLS if b in cubics or final]
        names |= {found[key][0] for key in used if key in found}
        names = sorted(names)
        made, shapes = {"arrays": []}, []
        for kind, members, number in (
            ("sum", [b for b in CELLS if b in squares and b not in finished], jnp.float32),
            ("square", finished, dtype),
            ("cubic", [b for b in CELLS if b in cubics and not final], jnp.float32),
        ):
            if members:
                made["arrays"].append(f"{kind}_{k}")
                shapes.append(tiles(len(members), number))
                made.update({(kind, b): (f"{kind}_{k}", place) for place, b in enumerate(members)})
        work, before = (squares, finished, cubics, final), dict(found)
        scratch = []
        if final:
            scratch = [pltpu.VMEM(shape.shape, shape.dtype) for shape in shapes]
            scratch += [pltpu.VMEM((9, 2, 3, width, width), dtype), pltpu.SemaphoreType.DMA((9, 2))]
        count = len(shapes)

        def body(*refs):
            if final:
                ins, out, rest = refs[: 2 + len(names)], refs[2 + len(names)], refs[3 + len(names) :]
                refs = (*ins, *rest[:count], out, *rest[count:])
            product_kernel(work, names, before, made, *refs)

        results = pl.pallas_call(
            body,
            out_shape=jax.ShapeDtypeStruct(blocks.shape, dtype) if final else shapes,
            in_specs=[smem, smem] + [vmem] * len(names),
            out_specs=hbm if final else [vmem] * count,
            scratch_shapes=scratch,
            compiler_params=pltpu.CompilerParams(vmem_limit_bytes=24 << 20),
            cost_estimate=pl.CostEstimate(flops=FLOPS[k], bytes_accessed=1, transcendentals=0),
            name=f"product{k}",
        )(flip, keep, *(arrays[name] for name in names))
        if final:
            return results
        arrays.update(zip(made["arrays"], results))
        found.update({key: place for key, place in made.items() if key != "arrays"})

    for event, gates in SCHEDULE:
        if isinstance(event, int):
            purified = multiply(event)
        else:
            move(event, gates)
    return purified[None, None]


def solution(mesh):
    return jax.shard_map(
        local,
        mesh=mesh,
        in_specs=(
            P(("grp", "row"), "col", None, None, None, None),
            P(("grp", "row"), "col", None, None),
        ),
        out_specs=P(("grp", "row"), "col", None, None, None, None),
        check_vma=False,
    )
```

```python
import jax
import jax.numpy as jnp
from jax import lax
from jax.experimental import pallas as pl
from jax.experimental.pallas import tpu as pltpu
from jax.sharding import PartitionSpec as P

STEPS = (-1, 0, 1)
CELLS = [(along_u, along_y) for along_u in STEPS for along_y in STEPS]
EDGES = {
    1: {"in": [(u, y) for u in (0, 1) for y in STEPS]},
    -1: {"in": [(u, y) for u in (0, -1) for y in STEPS]},
}
PIECES = {
    1: {"up": [(0, 0), (0, 1), (1, 0), (1, 1)], "up_rest": [(-1, 0), (-1, 1)]},
    -1: {"down0": [(0, -1), (0, 0)], "down1": [(1, -1), (1, 0)], "down2": [(-1, -1), (-1, 0)]},
}
STAGES = [['mat', 'x_in', 'up', 'x_up', 'down1', 'down0'],
 ['up_rest', 'down2', 'x_down0', 'x_down1', 'n_in', 'n_up', 'n_down0', 'n_down2', 'n_up_rest']]
SCHEDULE = [('x_in', []), ('up', []), ('x_up', []), ('down0', ['up']), ('up_rest', ['x_in']), ('down1', ['up']), (0, []),
 ('down2', ['x_in']), ('x_down0', []), ('x_down1', ['down1']), ('n_in', ['down0']), ('n_up', ['down0']),
 ('n_down0', ['sum_0']), ('n_down2', ['sum_0']), ('n_up_rest', ['down1', 'n_up', 'sum_0', 'x_down0']),
 (1, [])]


def holder(a, c):
    (au, ay), (cu, cy) = a, c
    if au == 0 and ay == 0:
        return "mat", CELLS.index(c)
    prefix = {0: "", 1: "x_", -1: "n_"}[au]
    wanted = (cu if au == 0 else -cu, cy)
    for name, tiles in (EDGES[au] if ay == 0 else PIECES[-ay]).items():
        if wanted in tiles:
            return prefix + name, tiles.index(wanted)


def pairs(b):
    for a in CELLS:
        c = (b[0] - a[0], b[1] - a[1])
        if abs(c[0]) <= 1 and abs(c[1]) <= 1:
            yield a, holder(a, c)


def stage_plan():
    stage_of = {name: k for k, names in enumerate(STAGES) for name in names}
    whole = {b: max(stage_of[name] for _, (name, _) in pairs(b)) for b in CELLS}
    plan = []
    for k in range(len(STAGES)):
        squares = {b: [p for p in pairs(b) if stage_of[p[1][0]] == k] for b in CELLS}
        cubics = {b: [p for p in pairs(b) if max(stage_of[p[1][0]], whole[p[0]]) == k] for b in CELLS}
        plan.append(
            (
                {b: chosen for b, chosen in squares.items() if chosen},
                [b for b in CELLS if whole[b] == k],
                {b: chosen for b, chosen in cubics.items() if chosen},
            )
        )
    return plan


def total(lefts, rights, base):
    summed = jnp.dot(
        jnp.concatenate(lefts, axis=1), jnp.concatenate(rights, axis=0), preferred_element_type=jnp.float32
    )
    return summed if base is None else base + summed


def far_side():
    return 2 * lax.rem(lax.axis_index("row"), 2) - 1


def first_slot(b, sign):
    return 3 * ((sign * b[0] + 1) * 3 + b[1] + 1)


def masked(block, kept):
    parts = block.reshape(block.shape[0] // kept.shape[0], *kept.shape)
    return (parts * kept.astype(block.dtype)[None]).reshape(block.shape)


def quarters(b, sign, mask, width):
    for low in range(2):
        for high in range(2):
            rows, columns = slice(low * width, (low + 1) * width), slice(high * width, (high + 1) * width)
            yield low, high, rows, columns, mask[low, first_slot(b, sign) + 1 + high - low]


def pack_kernel(layout, mask, values, *outs):
    width = values.shape[-1]
    sign = far_side()
    for b in CELLS:
        targets = [out.at[tiles.index(b)] for out, tiles in zip(outs, layout) if b in tiles]
        if not targets:
            continue
        for low, high, rows, columns, kept in quarters(b, sign, mask, width):
            block = masked(values[low, first_slot(b, sign) + 1 + high - low], kept)
            for target in targets:
                target[rows, columns] = block


def product_kernel(work, names, found, made, *refs):
    squares, finished, cubics, final = work
    inputs, refs = dict(zip(names, refs)), refs[len(names) :]
    outputs = dict(zip(made["arrays"], refs))
    sign, mask = far_side(), inputs.get("mask")

    def put(kind, b, value):
        name, place = made[kind, b]
        outputs[name][place] = value.astype(outputs[name].dtype)

    def get(kind, b):
        name, place = made[kind, b] if kind == "square" and ("square", b) in made else found[kind, b]
        return (outputs if name in outputs else inputs)[name][place]

    for b in CELLS:
        if b in squares or b in finished:
            base = get("sum", b) if ("sum", b) in found else None
            chosen = squares.get(b, [])
            value = base
            if chosen:
                lefts = [inputs["mat"][CELLS.index(a)] for a, _ in chosen]
                value = total(lefts, [inputs[name][place] for _, (name, place) in chosen], base)
            if b not in finished:
                put("sum", b, value)
                continue
            name, place = made["square", b]
            width = value.shape[-1] // 2
            for _, _, rows, columns, kept in quarters(b, sign, mask, width):
                outputs[name][place, rows, columns] = masked(value[rows, columns], kept).astype(outputs[name].dtype)
    if final:
        out, stage, copied = refs[len(outputs) :]
        width = out.shape[-1]
        empty = jnp.zeros((width, width), out.dtype)
        copies = []
    for b in CELLS:
        chosen = cubics.get(b, [])
        if not chosen and not final:
            continue
        value = get("cubic", b) if ("cubic", b) in found else None
        if chosen:
            lefts = [get("square", a) for a, _ in chosen]
            value = total(lefts, [inputs[name][place] for _, (name, place) in chosen], value)
        if not final:
            put("cubic", b, value)
            continue
        own = get("square", b).astype(jnp.float32)
        cell = CELLS.index(b)
        for low, high, rows, columns, kept in quarters(b, sign, mask, width):
            mixed = masked(3.0 * own[rows, columns] - 2.0 * value[rows, columns], kept)
            stage[cell, low, 1 + high - low] = mixed.astype(out.dtype)
        for low in range(2):
            stage[cell, low, 2 * low] = empty
            copies.append(
                pltpu.make_async_copy(
                    stage.at[cell, low], out.at[low, pl.ds(first_slot(b, sign), 3)], copied.at[cell, low]
                )
            )
            copies[-1].start()
    if final:
        for copy in copies:
            copy.wait()


def local(values, pattern):
    blocks, keep = values[0, 0], pattern[0, 0]
    dtype, width = blocks.dtype, blocks.shape[-1]
    side = 2 * width
    rows, cols = lax.axis_size("row"), lax.axis_size("col")

    near, far = [], []
    for i in range(0, rows, 2):
        near += [(i, i + 1), (i + 1, i)]
        far += [(i + 1, (i + 2) % rows), ((i + 2) % rows, i + 1)]
    up = [(i, (i + 1) % cols) for i in range(cols)]
    down = [(i, (i - 1) % cols) for i in range(cols)]

    def tiles(count, kind=dtype):
        return jax.ShapeDtypeStruct((count, side, side), kind)

    vmem = pl.BlockSpec(memory_space=pltpu.VMEM)
    hbm = pl.BlockSpec(memory_space=pltpu.HBM)

    sent = {name: (held, "col", up) for name, held in PIECES[1].items()}
    sent |= {name: (held, "col", down) for name, held in PIECES[-1].items()}
    sent |= {"x_" + name: (held, "row", far) for name, held in EDGES[1].items()}
    sent |= {"n_" + name: (held, "row", near) for name, held in EDGES[-1].items()}
    mask = jnp.broadcast_to(keep.astype(dtype)[:, :, None, None], (*keep.shape, 16, width))
    layout = [CELLS] + [held for held, _, _ in sent.values()]
    packed = pl.pallas_call(
        lambda *refs: pack_kernel(layout, *refs),
        out_shape=[tiles(len(held)) for held in layout],
        in_specs=[vmem, vmem],
        out_specs=[vmem] * len(layout),
        compiler_params=pltpu.CompilerParams(vmem_limit_bytes=16 << 20),
        name="pack",
    )(mask, blocks)
    ready = dict(zip(sent, packed[1:]))
    arrays = {"mat": packed[0], "mask": mask}
    plan, found = stage_plan(), {}

    def move(name, gates):
        if name in sent:
            operand, (_, axis, towards) = ready[name], sent[name]
        else:
            operand, axis, towards = arrays[name[2:]], "row", far if name[0] == "x" else near
        gates = [gate for gate in gates if name in sent or gate != name[2:]]
        if gates:
            operand, *held = lax.optimization_barrier((operand, *(arrays[gate] for gate in gates)))
            arrays.update(zip(gates, held))
            if name not in sent:
                arrays[name[2:]] = operand
        arrays[name] = lax.ppermute(operand, axis, towards)

    def multiply(k):
        squares, finished, cubics = plan[k]
        final = k == len(plan) - 1
        names = {"mat"} | {name for chosen in (*squares.values(), *cubics.values()) for _, (name, _) in chosen}
        used = [("sum", b) for b in CELLS if b in squares or b in finished]
        used += [("square", a) for chosen in cubics.values() for a, _ in chosen]
        used += [("square", b) for b in CELLS if final] + [("cubic", b) for b in CELLS if b in cubics or final]
        names |= {found[key][0] for key in used if key in found}
        if finished or final:
            names.add("mask")
        names = sorted(names)
        made, shapes = {"arrays": []}, []
        for kind, members, number in (
            ("sum", [b for b in CELLS if b in squares and b not in finished], jnp.float32),
            ("square", finished, dtype),
            ("cubic", [b for b in CELLS if b in cubics and not final], jnp.float32),
        ):
            if members:
                made["arrays"].append(f"{kind}_{k}")
                shapes.append(tiles(len(members), number))
                made.update({(kind, b): (f"{kind}_{k}", place) for place, b in enumerate(members)})
        work, before = (squares, finished, cubics, final), dict(found)
        scratch = []
        if final:
            scratch = [pltpu.VMEM(shape.shape, shape.dtype) for shape in shapes]
            scratch += [pltpu.VMEM((9, 2, 3, width, width), dtype), pltpu.SemaphoreType.DMA((9, 2))]
        count = len(shapes)

        def body(*refs):
            if final:
                ins, out, rest = refs[: len(names)], refs[len(names)], refs[1 + len(names) :]
                refs = (*ins, *rest[:count], out, *rest[count:])
            product_kernel(work, names, before, made, *refs)

        results = pl.pallas_call(
            body,
            out_shape=jax.ShapeDtypeStruct(blocks.shape, dtype) if final else shapes,
            in_specs=[vmem] * len(names),
            out_specs=hbm if final else [vmem] * count,
            scratch_shapes=scratch,
            compiler_params=pltpu.CompilerParams(vmem_limit_bytes=24 << 20),
            cost_estimate=pl.CostEstimate(flops=1, bytes_accessed=1, transcendentals=0),
            name=f"product{k}",
        )(*(arrays[name] for name in names))
        if final:
            return results
        arrays.update(zip(made["arrays"], results))
        found.update({key: place for key, place in made.items() if key != "arrays"})

    for event, gates in SCHEDULE:
        if isinstance(event, int):
            purified = multiply(event)
        else:
            move(event, gates)
    return purified[None, None]


def solution(mesh):
    return jax.shard_map(
        local,
        mesh=mesh,
        in_specs=(
            P(("grp", "row"), "col", None, None, None, None),
            P(("grp", "row"), "col", None, None),
        ),
        out_specs=P(("grp", "row"), "col", None, None, None, None),
        check_vma=False,
    )
```

```python
import jax
import jax.numpy as jnp
from jax import lax
from jax.experimental import pallas as pl
from jax.experimental.pallas import tpu as pltpu
from jax.sharding import PartitionSpec as P

STEPS = (-1, 0, 1)
CELLS = [(along_u, along_y) for along_u in STEPS for along_y in STEPS]
EDGES = {
    1: {"in": [(u, y) for u in (0, 1) for y in STEPS]},
    -1: {"in": [(u, y) for u in (0, -1) for y in STEPS]},
}
PIECES = {
    1: {"up": [(0, 0), (0, 1), (1, 0), (1, 1)], "up_rest": [(-1, 0), (-1, 1)]},
    -1: {"down0": [(0, -1), (0, 0)], "down1": [(1, -1), (1, 0)], "down2": [(-1, -1), (-1, 0)]},
}
STAGES = [['mat', 'x_in', 'up', 'x_up', 'down1', 'down0'],
 ['up_rest', 'down2', 'x_down0', 'x_down1', 'n_in', 'n_up', 'n_down0', 'n_down2', 'n_up_rest']]
SCHEDULE = [('x_in', []), ('up', []), ('x_up', []), ('down0', ['up']), ('up_rest', ['x_in']), ('down1', ['up']), (0, []),
 ('down2', ['x_in']), ('x_down0', []), ('x_down1', ['down1']), ('n_in', ['down0']), ('n_up', ['down0']),
 ('n_down0', ['sum_0']), ('n_down2', ['sum_0']), ('n_up_rest', ['down1', 'n_up', 'sum_0', 'x_down0']),
 (1, [])]


def holder(a, c):
    (au, ay), (cu, cy) = a, c
    if au == 0 and ay == 0:
        return "mat", CELLS.index(c)
    prefix = {0: "", 1: "x_", -1: "n_"}[au]
    wanted = (cu if au == 0 else -cu, cy)
    for name, tiles in (EDGES[au] if ay == 0 else PIECES[-ay]).items():
        if wanted in tiles:
            return prefix + name, tiles.index(wanted)


def pairs(b):
    for a in CELLS:
        c = (b[0] - a[0], b[1] - a[1])
        if abs(c[0]) <= 1 and abs(c[1]) <= 1:
            yield a, holder(a, c)


def stage_plan():
    stage_of = {name: k for k, names in enumerate(STAGES) for name in names}
    whole = {b: max(stage_of[name] for _, (name, _) in pairs(b)) for b in CELLS}
    plan = []
    for k in range(len(STAGES)):
        squares = {b: [p for p in pairs(b) if stage_of[p[1][0]] == k] for b in CELLS}
        cubics = {b: [p for p in pairs(b) if max(stage_of[p[1][0]], whole[p[0]]) == k] for b in CELLS}
        plan.append(
            (
                {b: chosen for b, chosen in squares.items() if chosen},
                [b for b in CELLS if whole[b] == k],
                {b: chosen for b, chosen in cubics.items() if chosen},
            )
        )
    return plan


def total(lefts, rights, base):
    summed = jnp.dot(
        jnp.concatenate(lefts, axis=1), jnp.concatenate(rights, axis=0), preferred_element_type=jnp.float32
    )
    return summed if base is None else base + summed


def far_side():
    return 2 * lax.rem(lax.axis_index("row"), 2) - 1


def first_slot(b, sign):
    return 3 * ((sign * b[0] + 1) * 3 + b[1] + 1)


def masked(block, kept):
    parts = block.reshape(block.shape[0] // kept.shape[0], *kept.shape)
    return (parts * kept.astype(block.dtype)[None]).reshape(block.shape)


def quarters(b, sign, mask, width):
    for low in range(2):
        for high in range(2):
            rows, columns = slice(low * width, (low + 1) * width), slice(high * width, (high + 1) * width)
            yield low, high, rows, columns, mask[low, first_slot(b, sign) + 1 + high - low]


def pack_kernel(layout, mask, values, *outs):
    width = values.shape[-1]
    sign = far_side()
    for b in CELLS:
        targets = [out.at[tiles.index(b)] for out, tiles in zip(outs, layout) if b in tiles]
        if not targets:
            continue
        for low, high, rows, columns, kept in quarters(b, sign, mask, width):
            block = masked(values[low, first_slot(b, sign) + 1 + high - low], kept)
            for target in targets:
                target[rows, columns] = block


def product_kernel(work, names, found, made, *refs):
    squares, finished, cubics, final = work
    inputs, refs = dict(zip(names, refs)), refs[len(names) :]
    outputs = dict(zip(made["arrays"], refs))
    sign, mask = far_side(), inputs.get("mask")

    def put(kind, b, value):
        name, place = made[kind, b]
        outputs[name][place] = value.astype(outputs[name].dtype)

    def get(kind, b):
        name, place = made[kind, b] if kind == "square" and ("square", b) in made else found[kind, b]
        return (outputs if name in outputs else inputs)[name][place]

    for b in CELLS:
        if b in squares or b in finished:
            base = get("sum", b) if ("sum", b) in found else None
            chosen = squares.get(b, [])
            value = base
            if chosen:
                lefts = [inputs["mat"][CELLS.index(a)] for a, _ in chosen]
                value = total(lefts, [inputs[name][place] for _, (name, place) in chosen], base)
            if b not in finished:
                put("sum", b, value)
                continue
            name, place = made["square", b]
            width = value.shape[-1] // 2
            for _, _, rows, columns, kept in quarters(b, sign, mask, width):
                outputs[name][place, rows, columns] = masked(value[rows, columns], kept).astype(outputs[name].dtype)
    if final:
        out, stage, copied = refs[len(outputs) :]
        width = out.shape[-1]
        empty = jnp.zeros((width, width), out.dtype)
        copies = []
    for b in CELLS:
        chosen = cubics.get(b, [])
        if not chosen and not final:
            continue
        value = get("cubic", b) if ("cubic", b) in found else None
        if chosen:
            lefts = [get("square", a) for a, _ in chosen]
            value = total(lefts, [inputs[name][place] for _, (name, place) in chosen], value)
        if not final:
            put("cubic", b, value)
            continue
        own = get("square", b).astype(jnp.float32)
        cell = CELLS.index(b)
        for low, high, rows, columns, kept in quarters(b, sign, mask, width):
            mixed = masked(3.0 * own[rows, columns] - 2.0 * value[rows, columns], kept)
            stage[cell, low, 1 + high - low] = mixed.astype(out.dtype)
        for low in range(2):
            stage[cell, low, 2 * low] = empty
            copies.append(
                pltpu.make_async_copy(
                    stage.at[cell, low], out.at[low, pl.ds(first_slot(b, sign), 3)], copied.at[cell, low]
                )
            )
            copies[-1].start()
    if final:
        for copy in copies:
            copy.wait()


def local(values, pattern):
    blocks, keep = values[0, 0], pattern[0, 0]
    dtype, width = blocks.dtype, blocks.shape[-1]
    side = 2 * width
    rows, cols = lax.axis_size("row"), lax.axis_size("col")

    near, far = [], []
    for i in range(0, rows, 2):
        near += [(i, i + 1), (i + 1, i)]
        far += [(i + 1, (i + 2) % rows), ((i + 2) % rows, i + 1)]
    up = [(i, (i + 1) % cols) for i in range(cols)]
    down = [(i, (i - 1) % cols) for i in range(cols)]

    def tiles(count, kind=dtype):
        return jax.ShapeDtypeStruct((count, side, side), kind)

    vmem = pl.BlockSpec(memory_space=pltpu.VMEM)
    hbm = pl.BlockSpec(memory_space=pltpu.HBM)

    sent = {name: (held, "col", up) for name, held in PIECES[1].items()}
    sent |= {name: (held, "col", down) for name, held in PIECES[-1].items()}
    sent |= {"x_" + name: (held, "row", far) for name, held in EDGES[1].items()}
    sent |= {"n_" + name: (held, "row", near) for name, held in EDGES[-1].items()}
    mask = jnp.broadcast_to(keep.astype(dtype)[:, :, None, None], (*keep.shape, width, width))
    layout = [CELLS] + [held for held, _, _ in sent.values()]
    packed = pl.pallas_call(
        lambda *refs: pack_kernel(layout, *refs),
        out_shape=[tiles(len(held)) for held in layout],
        in_specs=[vmem, vmem],
        out_specs=[vmem] * len(layout),
        compiler_params=pltpu.CompilerParams(vmem_limit_bytes=16 << 20),
        name="pack",
    )(mask, blocks)
    ready = dict(zip(sent, packed[1:]))
    arrays = {"mat": packed[0], "mask": mask}
    plan, found = stage_plan(), {}

    def move(name, gates):
        if name in sent:
            operand, (_, axis, towards) = ready[name], sent[name]
        else:
            operand, axis, towards = arrays[name[2:]], "row", far if name[0] == "x" else near
        gates = [gate for gate in gates if name in sent or gate != name[2:]]
        if gates:
            operand, *held = lax.optimization_barrier((operand, *(arrays[gate] for gate in gates)))
            arrays.update(zip(gates, held))
            if name not in sent:
                arrays[name[2:]] = operand
        arrays[name] = lax.ppermute(operand, axis, towards)

    def multiply(k):
        squares, finished, cubics = plan[k]
        final = k == len(plan) - 1
        names = {"mat"} | {name for chosen in (*squares.values(), *cubics.values()) for _, (name, _) in chosen}
        used = [("sum", b) for b in CELLS if b in squares or b in finished]
        used += [("square", a) for chosen in cubics.values() for a, _ in chosen]
        used += [("square", b) for b in CELLS if final] + [("cubic", b) for b in CELLS if b in cubics or final]
        names |= {found[key][0] for key in used if key in found}
        if finished or final:
            names.add("mask")
        names = sorted(names)
        made, shapes = {"arrays": []}, []
        for kind, members, number in (
            ("sum", [b for b in CELLS if b in squares and b not in finished], jnp.float32),
            ("square", finished, dtype),
            ("cubic", [b for b in CELLS if b in cubics and not final], jnp.float32),
        ):
            if members:
                made["arrays"].append(f"{kind}_{k}")
                shapes.append(tiles(len(members), number))
                made.update({(kind, b): (f"{kind}_{k}", place) for place, b in enumerate(members)})
        work, before = (squares, finished, cubics, final), dict(found)
        scratch = []
        if final:
            scratch = [pltpu.VMEM(shape.shape, shape.dtype) for shape in shapes]
            scratch += [pltpu.VMEM((9, 2, 3, width, width), dtype), pltpu.SemaphoreType.DMA((9, 2))]
        count = len(shapes)

        def body(*refs):
            if final:
                ins, out, rest = refs[: len(names)], refs[len(names)], refs[1 + len(names) :]
                refs = (*ins, *rest[:count], out, *rest[count:])
            product_kernel(work, names, before, made, *refs)

        results = pl.pallas_call(
            body,
            out_shape=jax.ShapeDtypeStruct(blocks.shape, dtype) if final else shapes,
            in_specs=[vmem] * len(names),
            out_specs=hbm if final else [vmem] * count,
            scratch_shapes=scratch,
            compiler_params=pltpu.CompilerParams(vmem_limit_bytes=24 << 20),
            cost_estimate=pl.CostEstimate(flops=1, bytes_accessed=1, transcendentals=0),
            name=f"product{k}",
        )(*(arrays[name] for name in names))
        if final:
            return results
        arrays.update(zip(made["arrays"], results))
        found.update({key: place for key, place in made.items() if key != "arrays"})

    for event, gates in SCHEDULE:
        if isinstance(event, int):
            purified = multiply(event)
        else:
            move(event, gates)
    return purified[None, None]


def solution(mesh):
    return jax.shard_map(
        local,
        mesh=mesh,
        in_specs=(
            P(("grp", "row"), "col", None, None, None, None),
            P(("grp", "row"), "col", None, None),
        ),
        out_specs=P(("grp", "row"), "col", None, None, None, None),
        check_vma=False,
    )
```

```python
import jax
import jax.numpy as jnp
from jax import lax
from jax.experimental import pallas as pl
from jax.experimental.pallas import tpu as pltpu
from jax.sharding import PartitionSpec as P

STEPS = (-1, 0, 1)
CELLS = [(along_u, along_y) for along_u in STEPS for along_y in STEPS]
EDGES = {
    1: {"in": [(u, y) for u in (0, 1) for y in STEPS]},
    -1: {"in": [(u, y) for u in (0, -1) for y in STEPS]},
}
PIECES = {
    1: {"up": [(0, 0), (0, 1), (1, 0), (1, 1)], "up_rest": [(-1, 0), (-1, 1)]},
    -1: {"down0": [(0, -1), (0, 0)], "down1": [(1, -1), (1, 0)], "down2": [(-1, -1), (-1, 0)]},
}
STAGES = [['mat', 'x_in', 'x_up'], ['up', 'down1'],
 ['up_rest', 'down2', 'x_down0', 'x_down1', 'n_in', 'n_up', 'n_down2', 'down0', 'n_down0', 'n_up_rest']]
SCHEDULE = [('x_in', []), ('up', []), ('x_up', []), (0, []), ('down0', ['up']), ('down1', ['up']), (1, []),
 ('up_rest', ['x_in']), ('down2', ['x_in']), ('x_down0', []), ('x_down1', ['x_up']), ('n_in', []),
 ('n_up', ['down0', 'n_in']), ('n_down0', ['sum_0', 'x_in']), ('n_down2', ['sum_0']),
 ('n_up_rest', ['down1', 'n_up', 'sum_0', 'x_down0']), (2, [])]


def holder(a, c):
    (au, ay), (cu, cy) = a, c
    if au == 0 and ay == 0:
        return "mat", CELLS.index(c)
    prefix = {0: "", 1: "x_", -1: "n_"}[au]
    wanted = (cu if au == 0 else -cu, cy)
    for name, tiles in (EDGES[au] if ay == 0 else PIECES[-ay]).items():
        if wanted in tiles:
            return prefix + name, tiles.index(wanted)


def pairs(b):
    for a in CELLS:
        c = (b[0] - a[0], b[1] - a[1])
        if abs(c[0]) <= 1 and abs(c[1]) <= 1:
            yield a, holder(a, c)


def stage_plan():
    stage_of = {name: k for k, names in enumerate(STAGES) for name in names}
    whole = {b: max(stage_of[name] for _, (name, _) in pairs(b)) for b in CELLS}
    plan = []
    for k in range(len(STAGES)):
        squares = {b: [p for p in pairs(b) if stage_of[p[1][0]] == k] for b in CELLS}
        cubics = {b: [p for p in pairs(b) if max(stage_of[p[1][0]], whole[p[0]]) == k] for b in CELLS}
        plan.append(
            (
                {b: chosen for b, chosen in squares.items() if chosen},
                [b for b in CELLS if whole[b] == k],
                {b: chosen for b, chosen in cubics.items() if chosen},
            )
        )
    return plan


def total(lefts, rights, base):
    summed = jnp.dot(
        jnp.concatenate(lefts, axis=1), jnp.concatenate(rights, axis=0), preferred_element_type=jnp.float32
    )
    return summed if base is None else base + summed


def far_side():
    return 2 * lax.rem(lax.axis_index("row"), 2) - 1


def first_slot(b, sign):
    return 3 * ((sign * b[0] + 1) * 3 + b[1] + 1)


def masked(block, kept):
    parts = block.reshape(block.shape[0] // kept.shape[0], *kept.shape)
    return (parts * kept.astype(block.dtype)[None]).reshape(block.shape)


def quarters(b, sign, mask, width):
    for low in range(2):
        for high in range(2):
            rows, columns = slice(low * width, (low + 1) * width), slice(high * width, (high + 1) * width)
            yield low, high, rows, columns, mask[low, first_slot(b, sign) + 1 + high - low]


def pack_kernel(layout, mask, values, *outs):
    width = values.shape[-1]
    sign = far_side()
    for b in CELLS:
        targets = [out.at[tiles.index(b)] for out, tiles in zip(outs, layout) if b in tiles]
        if not targets:
            continue
        for low, high, rows, columns, kept in quarters(b, sign, mask, width):
            block = masked(values[low, first_slot(b, sign) + 1 + high - low], kept)
            for target in targets:
                target[rows, columns] = block


def product_kernel(work, names, found, made, *refs):
    squares, finished, cubics, final = work
    inputs, refs = dict(zip(names, refs)), refs[len(names) :]
    outputs = dict(zip(made["arrays"], refs))
    sign, mask = far_side(), inputs.get("mask")

    def put(kind, b, value):
        name, place = made[kind, b]
        outputs[name][place] = value.astype(outputs[name].dtype)

    def get(kind, b):
        name, place = made[kind, b] if kind == "square" and ("square", b) in made else found[kind, b]
        return (outputs if name in outputs else inputs)[name][place]

    for b in CELLS:
        if b in squares or b in finished:
            base = get("sum", b) if ("sum", b) in found else None
            chosen = squares.get(b, [])
            value = base
            if chosen:
                lefts = [inputs["mat"][CELLS.index(a)] for a, _ in chosen]
                value = total(lefts, [inputs[name][place] for _, (name, place) in chosen], base)
            if b not in finished:
                put("sum", b, value)
                continue
            name, place = made["square", b]
            width = value.shape[-1] // 2
            for _, _, rows, columns, kept in quarters(b, sign, mask, width):
                outputs[name][place, rows, columns] = masked(value[rows, columns], kept).astype(outputs[name].dtype)
    if final:
        out, stage, copied = refs[len(outputs) :]
        width = out.shape[-1]
        empty = jnp.zeros((width, width), out.dtype)
        copies = []
    for b in CELLS:
        chosen = cubics.get(b, [])
        if not chosen and not final:
            continue
        value = get("cubic", b) if ("cubic", b) in found else None
        if chosen:
            lefts = [get("square", a) for a, _ in chosen]
            value = total(lefts, [inputs[name][place] for _, (name, place) in chosen], value)
        if not final:
            put("cubic", b, value)
            continue
        own = get("square", b).astype(jnp.float32)
        cell = CELLS.index(b)
        for low, high, rows, columns, kept in quarters(b, sign, mask, width):
            mixed = masked(3.0 * own[rows, columns] - 2.0 * value[rows, columns], kept)
            stage[cell, low, 1 + high - low] = mixed.astype(out.dtype)
        for low in range(2):
            stage[cell, low, 2 * low] = empty
            copies.append(
                pltpu.make_async_copy(
                    stage.at[cell, low], out.at[low, pl.ds(first_slot(b, sign), 3)], copied.at[cell, low]
                )
            )
            copies[-1].start()
    if final:
        for copy in copies:
            copy.wait()


def local(values, pattern):
    blocks, keep = values[0, 0], pattern[0, 0]
    dtype, width = blocks.dtype, blocks.shape[-1]
    side = 2 * width
    rows, cols = lax.axis_size("row"), lax.axis_size("col")

    near, far = [], []
    for i in range(0, rows, 2):
        near += [(i, i + 1), (i + 1, i)]
        far += [(i + 1, (i + 2) % rows), ((i + 2) % rows, i + 1)]
    up = [(i, (i + 1) % cols) for i in range(cols)]
    down = [(i, (i - 1) % cols) for i in range(cols)]

    def tiles(count, kind=dtype):
        return jax.ShapeDtypeStruct((count, side, side), kind)

    vmem = pl.BlockSpec(memory_space=pltpu.VMEM)
    hbm = pl.BlockSpec(memory_space=pltpu.HBM)

    sent = {name: (held, "col", up) for name, held in PIECES[1].items()}
    sent |= {name: (held, "col", down) for name, held in PIECES[-1].items()}
    sent |= {"x_" + name: (held, "row", far) for name, held in EDGES[1].items()}
    sent |= {"n_" + name: (held, "row", near) for name, held in EDGES[-1].items()}
    mask = jnp.broadcast_to(keep.astype(dtype)[:, :, None, None], (*keep.shape, width, width))
    layout = [CELLS] + [held for held, _, _ in sent.values()]
    packed = pl.pallas_call(
        lambda *refs: pack_kernel(layout, *refs),
        out_shape=[tiles(len(held)) for held in layout],
        in_specs=[vmem, vmem],
        out_specs=[vmem] * len(layout),
        compiler_params=pltpu.CompilerParams(vmem_limit_bytes=16 << 20),
        name="pack",
    )(mask, blocks)
    ready = dict(zip(sent, packed[1:]))
    arrays = {"mat": packed[0], "mask": mask}
    plan, found = stage_plan(), {}

    def move(name, gates):
        if name in sent:
            operand, (_, axis, towards) = ready[name], sent[name]
        else:
            operand, axis, towards = arrays[name[2:]], "row", far if name[0] == "x" else near
        gates = [gate for gate in gates if name in sent or gate != name[2:]]
        if gates:
            operand, *held = lax.optimization_barrier((operand, *(arrays[gate] for gate in gates)))
            arrays.update(zip(gates, held))
            if name not in sent:
                arrays[name[2:]] = operand
        arrays[name] = lax.ppermute(operand, axis, towards)

    def multiply(k):
        squares, finished, cubics = plan[k]
        final = k == len(plan) - 1
        names = {"mat"} | {name for chosen in (*squares.values(), *cubics.values()) for _, (name, _) in chosen}
        used = [("sum", b) for b in CELLS if b in squares or b in finished]
        used += [("square", a) for chosen in cubics.values() for a, _ in chosen]
        used += [("square", b) for b in CELLS if final] + [("cubic", b) for b in CELLS if b in cubics or final]
        names |= {found[key][0] for key in used if key in found}
        if finished or final:
            names.add("mask")
        names = sorted(names)
        made, shapes = {"arrays": []}, []
        for kind, members, number in (
            ("sum", [b for b in CELLS if b in squares and b not in finished], jnp.float32),
            ("square", finished, dtype),
            ("cubic", [b for b in CELLS if b in cubics and not final], jnp.float32),
        ):
            if members:
                made["arrays"].append(f"{kind}_{k}")
                shapes.append(tiles(len(members), number))
                made.update({(kind, b): (f"{kind}_{k}", place) for place, b in enumerate(members)})
        work, before = (squares, finished, cubics, final), dict(found)
        scratch = []
        if final:
            scratch = [pltpu.VMEM(shape.shape, shape.dtype) for shape in shapes]
            scratch += [pltpu.VMEM((9, 2, 3, width, width), dtype), pltpu.SemaphoreType.DMA((9, 2))]
        count = len(shapes)

        def body(*refs):
            if final:
                ins, out, rest = refs[: len(names)], refs[len(names)], refs[1 + len(names) :]
                refs = (*ins, *rest[:count], out, *rest[count:])
            product_kernel(work, names, before, made, *refs)

        results = pl.pallas_call(
            body,
            out_shape=jax.ShapeDtypeStruct(blocks.shape, dtype) if final else shapes,
            in_specs=[vmem] * len(names),
            out_specs=hbm if final else [vmem] * count,
            scratch_shapes=scratch,
            compiler_params=pltpu.CompilerParams(vmem_limit_bytes=24 << 20),
            cost_estimate=pl.CostEstimate(flops=1, bytes_accessed=1, transcendentals=0),
            name=f"product{k}",
        )(*(arrays[name] for name in names))
        if final:
            return results
        arrays.update(zip(made["arrays"], results))
        found.update({key: place for key, place in made.items() if key != "arrays"})

    for event, gates in SCHEDULE:
        if isinstance(event, int):
            purified = multiply(event)
        else:
            move(event, gates)
    return purified[None, None]


def solution(mesh):
    return jax.shard_map(
        local,
        mesh=mesh,
        in_specs=(
            P(("grp", "row"), "col", None, None, None, None),
            P(("grp", "row"), "col", None, None),
        ),
        out_specs=P(("grp", "row"), "col", None, None, None, None),
        check_vma=False,
    )
```

```python
import jax
import jax.numpy as jnp
from jax import lax
from jax.experimental import pallas as pl
from jax.experimental.pallas import tpu as pltpu
from jax.sharding import PartitionSpec as P

STEPS = (-1, 0, 1)
CELLS = [(along_u, along_y) for along_u in STEPS for along_y in STEPS]
EDGES = {
    1: {"in": [(u, y) for u in (0, 1) for y in STEPS]},
    -1: {"in": [(u, y) for u in (0, -1) for y in STEPS]},
}
PIECES = {
    1: {"up": [(0, 0), (0, 1), (1, 0), (1, 1)], "up_rest": [(-1, 0), (-1, 1)]},
    -1: {"down0": [(0, -1), (0, 0)], "down1": [(1, -1), (1, 0)], "down2": [(-1, -1), (-1, 0)]},
}
STAGES = [
    ["mat", "x_in", "x_up"],
    ["up", "down1", "down0"],
    ["up_rest", "down2", "x_down0", "x_down1", "n_in", "n_up", "n_down2", "n_down0", "n_up_rest"],
]
SCHEDULE = [('x_in', []), ('up', []), ('x_up', []), (0, []), ('down0', ['up']), ('down1', ['up']), (1, []),
 ('up_rest', ['x_in']), ('down2', ['x_in']), ('x_down0', []), ('x_down1', ['x_up']), ('n_in', []),
 ('n_up', ['down0', 'n_in']), ('n_down0', ['sum_0', 'x_in']), ('n_down2', ['sum_0']),
 ('n_up_rest', ['down1', 'n_up', 'sum_0', 'x_down0']), (2, [])]


def holder(a, c):
    (au, ay), (cu, cy) = a, c
    if au == 0 and ay == 0:
        return "mat", CELLS.index(c)
    prefix = {0: "", 1: "x_", -1: "n_"}[au]
    wanted = (cu if au == 0 else -cu, cy)
    for name, tiles in (EDGES[au] if ay == 0 else PIECES[-ay]).items():
        if wanted in tiles:
            return prefix + name, tiles.index(wanted)


def pairs(b):
    for a in CELLS:
        c = (b[0] - a[0], b[1] - a[1])
        if abs(c[0]) <= 1 and abs(c[1]) <= 1:
            yield a, holder(a, c)


def stage_plan():
    stage_of = {name: k for k, names in enumerate(STAGES) for name in names}
    whole = {b: max(stage_of[name] for _, (name, _) in pairs(b)) for b in CELLS}
    plan = []
    for k in range(len(STAGES)):
        squares = {b: [p for p in pairs(b) if stage_of[p[1][0]] == k] for b in CELLS}
        cubics = {b: [p for p in pairs(b) if max(stage_of[p[1][0]], whole[p[0]]) == k] for b in CELLS}
        plan.append(
            (
                {b: chosen for b, chosen in squares.items() if chosen},
                [b for b in CELLS if whole[b] == k],
                {b: chosen for b, chosen in cubics.items() if chosen},
            )
        )
    return plan


def total(lefts, rights, base):
    summed = jnp.dot(
        jnp.concatenate(lefts, axis=1), jnp.concatenate(rights, axis=0), preferred_element_type=jnp.float32
    )
    return summed if base is None else base + summed


def far_side():
    return 2 * lax.rem(lax.axis_index("row"), 2) - 1


def first_slot(b, sign):
    return 3 * ((sign * b[0] + 1) * 3 + b[1] + 1)


def masked(block, kept):
    parts = block.reshape(block.shape[0] // kept.shape[0], *kept.shape)
    return (parts * kept.astype(block.dtype)[None]).reshape(block.shape)


def quarters(b, sign, mask, width):
    for low in range(2):
        for high in range(2):
            rows, columns = slice(low * width, (low + 1) * width), slice(high * width, (high + 1) * width)
            yield low, high, rows, columns, mask[low, first_slot(b, sign) + 1 + high - low]


def pack_kernel(layout, mask, values, *outs):
    width = values.shape[-1]
    sign = far_side()
    for b in CELLS:
        targets = [out.at[tiles.index(b)] for out, tiles in zip(outs, layout) if b in tiles]
        if not targets:
            continue
        for low, high, rows, columns, kept in quarters(b, sign, mask, width):
            block = masked(values[low, first_slot(b, sign) + 1 + high - low], kept)
            for target in targets:
                target[rows, columns] = block


def product_kernel(work, names, found, made, *refs):
    squares, finished, cubics, final = work
    inputs, refs = dict(zip(names, refs)), refs[len(names) :]
    outputs = dict(zip(made["arrays"], refs))
    sign, mask = far_side(), inputs.get("mask")

    def put(kind, b, value):
        name, place = made[kind, b]
        outputs[name][place] = value.astype(outputs[name].dtype)

    def get(kind, b):
        name, place = made[kind, b] if kind == "square" and ("square", b) in made else found[kind, b]
        return (outputs if name in outputs else inputs)[name][place]

    for b in CELLS:
        if b in squares or b in finished:
            base = get("sum", b) if ("sum", b) in found else None
            chosen = squares.get(b, [])
            value = base
            if chosen:
                lefts = [inputs["mat"][CELLS.index(a)] for a, _ in chosen]
                value = total(lefts, [inputs[name][place] for _, (name, place) in chosen], base)
            if b not in finished:
                put("sum", b, value)
                continue
            name, place = made["square", b]
            width = value.shape[-1] // 2
            for _, _, rows, columns, kept in quarters(b, sign, mask, width):
                outputs[name][place, rows, columns] = masked(value[rows, columns], kept).astype(outputs[name].dtype)
    if final:
        out, stage, copied = refs[len(outputs) :]
        width = out.shape[-1]
        empty = jnp.zeros((width, width), out.dtype)
        copies = []
    for b in CELLS:
        chosen = cubics.get(b, [])
        if not chosen and not final:
            continue
        value = get("cubic", b) if ("cubic", b) in found else None
        if chosen:
            lefts = [get("square", a) for a, _ in chosen]
            value = total(lefts, [inputs[name][place] for _, (name, place) in chosen], value)
        if not final:
            put("cubic", b, value)
            continue
        own = get("square", b).astype(jnp.float32)
        cell = CELLS.index(b)
        for low, high, rows, columns, kept in quarters(b, sign, mask, width):
            mixed = masked(3.0 * own[rows, columns] - 2.0 * value[rows, columns], kept)
            stage[cell, low, 1 + high - low] = mixed.astype(out.dtype)
        for low in range(2):
            stage[cell, low, 2 * low] = empty
            copies.append(
                pltpu.make_async_copy(
                    stage.at[cell, low], out.at[low, pl.ds(first_slot(b, sign), 3)], copied.at[cell, low]
                )
            )
            copies[-1].start()
    if final:
        for copy in copies:
            copy.wait()


def local(values, pattern):
    blocks, keep = values[0, 0], pattern[0, 0]
    dtype, width = blocks.dtype, blocks.shape[-1]
    side = 2 * width
    rows, cols = lax.axis_size("row"), lax.axis_size("col")

    near, far = [], []
    for i in range(0, rows, 2):
        near += [(i, i + 1), (i + 1, i)]
        far += [(i + 1, (i + 2) % rows), ((i + 2) % rows, i + 1)]
    up = [(i, (i + 1) % cols) for i in range(cols)]
    down = [(i, (i - 1) % cols) for i in range(cols)]

    def tiles(count, kind=dtype):
        return jax.ShapeDtypeStruct((count, side, side), kind)

    vmem = pl.BlockSpec(memory_space=pltpu.VMEM)
    hbm = pl.BlockSpec(memory_space=pltpu.HBM)

    sent = {name: (held, "col", up) for name, held in PIECES[1].items()}
    sent |= {name: (held, "col", down) for name, held in PIECES[-1].items()}
    sent |= {"x_" + name: (held, "row", far) for name, held in EDGES[1].items()}
    sent |= {"n_" + name: (held, "row", near) for name, held in EDGES[-1].items()}
    mask = jnp.broadcast_to(keep.astype(dtype)[:, :, None, None], (*keep.shape, width, width))
    layout = [CELLS] + [held for held, _, _ in sent.values()]
    packed = pl.pallas_call(
        lambda *refs: pack_kernel(layout, *refs),
        out_shape=[tiles(len(held)) for held in layout],
        in_specs=[vmem, vmem],
        out_specs=[vmem] * len(layout),
        compiler_params=pltpu.CompilerParams(vmem_limit_bytes=16 << 20),
        name="pack",
    )(mask, blocks)
    ready = dict(zip(sent, packed[1:]))
    arrays = {"mat": packed[0], "mask": mask}
    plan, found = stage_plan(), {}

    def move(name, gates):
        if name in sent:
            operand, (_, axis, towards) = ready[name], sent[name]
        else:
            operand, axis, towards = arrays[name[2:]], "row", far if name[0] == "x" else near
        gates = [gate for gate in gates if name in sent or gate != name[2:]]
        if gates:
            operand, *held = lax.optimization_barrier((operand, *(arrays[gate] for gate in gates)))
            arrays.update(zip(gates, held))
            if name not in sent:
                arrays[name[2:]] = operand
        arrays[name] = lax.ppermute(operand, axis, towards)

    def multiply(k):
        squares, finished, cubics = plan[k]
        final = k == len(plan) - 1
        names = {"mat"} | {name for chosen in (*squares.values(), *cubics.values()) for _, (name, _) in chosen}
        used = [("sum", b) for b in CELLS if b in squares or b in finished]
        used += [("square", a) for chosen in cubics.values() for a, _ in chosen]
        used += [("square", b) for b in CELLS if final] + [("cubic", b) for b in CELLS if b in cubics or final]
        names |= {found[key][0] for key in used if key in found}
        if finished or final:
            names.add("mask")
        names = sorted(names)
        made, shapes = {"arrays": []}, []
        for kind, members, number in (
            ("sum", [b for b in CELLS if b in squares and b not in finished], jnp.float32),
            ("square", finished, dtype),
            ("cubic", [b for b in CELLS if b in cubics and not final], jnp.float32),
        ):
            if members:
                made["arrays"].append(f"{kind}_{k}")
                shapes.append(tiles(len(members), number))
                made.update({(kind, b): (f"{kind}_{k}", place) for place, b in enumerate(members)})
        work, before = (squares, finished, cubics, final), dict(found)
        scratch = []
        if final:
            scratch = [pltpu.VMEM(shape.shape, shape.dtype) for shape in shapes]
            scratch += [pltpu.VMEM((9, 2, 3, width, width), dtype), pltpu.SemaphoreType.DMA((9, 2))]
        count = len(shapes)

        def body(*refs):
            if final:
                ins, out, rest = refs[: len(names)], refs[len(names)], refs[1 + len(names) :]
                refs = (*ins, *rest[:count], out, *rest[count:])
            product_kernel(work, names, before, made, *refs)

        results = pl.pallas_call(
            body,
            out_shape=jax.ShapeDtypeStruct(blocks.shape, dtype) if final else shapes,
            in_specs=[vmem] * len(names),
            out_specs=hbm if final else [vmem] * count,
            scratch_shapes=scratch,
            compiler_params=pltpu.CompilerParams(vmem_limit_bytes=24 << 20),
            cost_estimate=pl.CostEstimate(flops=1, bytes_accessed=1, transcendentals=0),
            name=f"product{k}",
        )(*(arrays[name] for name in names))
        if final:
            return results
        arrays.update(zip(made["arrays"], results))
        found.update({key: place for key, place in made.items() if key != "arrays"})

    for event, gates in SCHEDULE:
        if isinstance(event, int):
            purified = multiply(event)
        else:
            move(event, gates)
    return purified[None, None]


def solution(mesh):
    return jax.shard_map(
        local,
        mesh=mesh,
        in_specs=(
            P(("grp", "row"), "col", None, None, None, None),
            P(("grp", "row"), "col", None, None),
        ),
        out_specs=P(("grp", "row"), "col", None, None, None, None),
        check_vma=False,
    )
```
